768 devices in a mesh: fsdp: 64 (over y, x, core), tp: 12 (over z).
Axes of the slice: x: 4, y: 8, z: 12, core: 2. Of those that a mesh axis runs over, the one named last changes fastest.
Arguments:
- momentum: float32 [8192, 27648], P('fsdp', 'tp'), may hold values from -60 to 60
- gradient: bfloat16 [8192, 27648], P('fsdp', 'tp'), may hold values from -6 to 6
- right_factor: float32 [256, 27648], P('fsdp', 'tp'), may hold values from -6 to 6
Outputs:
- next_momentum: float32 [8192, 27648], P('fsdp', 'tp')
- update: bfloat16 [8192, 27648], P('fsdp', 'tp')
- next_factor: float32 [256, 27648], P('fsdp', 'tp')
The draws below stay inside these ranges and needn't reach their ends.
All inputs are finite; a program needn't handle non-finite values.
Results may differ from the reference program's by a relative error of at most 0.001.
Values sent between devices are 32-bit elements; how exact they have to be, the bound alone decides.
A program may use at most 32 MiB of HBM per device.

```python
import math
import jax
import jax.numpy as jnp
from jax import lax

ROWS = 8192
COLS = 27648
RANK = 256


def draw_momentum(key, part):
    key = jax.random.fold_in(key, 7)
    first, second, third = jax.random.split(key, 3)
    base = jax.random.normal(first, (ROWS, COLS), jnp.float32)
    lower, upper = (0.3, 3.0)
    row_scale = jnp.exp(jax.random.uniform(second, (ROWS, 1), jnp.float32, math.log(lower), math.log(upper)))
    col_scale = jnp.exp(jax.random.uniform(third, (1, COLS), jnp.float32, math.log(lower), math.log(upper)))
    return jnp.clip(base * row_scale * col_scale, -60.0, 60.0)


def block_scale(own_key, extent, cuts, low, top_value):
    def one(dim, parts):
        heights = jax.random.uniform(jax.random.fold_in(jax.random.fold_in(own_key, 6), dim), (parts,), jnp.float32, low / len(cuts), top_value / len(cuts))
        return jnp.repeat(jnp.exp(heights), extent[dim] // parts).reshape((-1,) + (1,) * (len(extent) - dim - 1))

    factor_of = one(*cuts[0])
    for cut in cuts[1:]:
        factor_of = factor_of * one(*cut)
    return factor_of


def scatter_about(rng, extent, deviation, most, shards=(), dtype=jnp.bfloat16):
    array = deviation * jax.random.normal(rng, extent, jnp.float32)
    if shards:
        array = array * block_scale(rng, extent, shards, -0.22, 0.18)
    return jnp.clip(array, -most, most).astype(dtype)


def setup_inputs(seed: int = 0) -> dict:
    arg_keys = jax.random.split(jax.random.key(seed), 4)
    momentum = draw_momentum(jax.random.fold_in(arg_keys[3], 71), 0)
    gradient = scatter_about(arg_keys[1], (ROWS, COLS), 1.0, 6.0, ((0, 64), (1, 12)))
    right_factor = scatter_about(arg_keys[2], (RANK, COLS), 1.0, 6.0, ((0, 64), (1, 12)), jnp.float32)
    return dict(momentum=momentum, gradient=gradient, right_factor=right_factor)


decay_rate = 0.9
norm_eps = 1e-08

def reference(momentum, gradient, right_factor):
    highest = lax.Precision.HIGHEST
    buffer = momentum + gradient.astype(jnp.float32)
    left_factor = jnp.dot(buffer, right_factor.T, precision=highest)
    gram = jnp.dot(left_factor.T, left_factor, precision=highest)
    lower_factor = jnp.linalg.cholesky(gram)
    left_basis = jax.scipy.linalg.solve_triangular(lower_factor, left_factor.T, lower=True).T
    right_rows = jnp.dot(left_basis.T, buffer, precision=highest)
    inverse_norm = 1.0 / (jnp.sqrt(lax.optimization_barrier(jnp.sum(right_rows * right_rows, axis=1))) + norm_eps)
    next_factor = right_rows * inverse_norm[:, None]
    next_momentum = buffer - (1.0 - decay_rate) * jnp.dot(left_basis, right_rows, precision=highest)
    update_scale = math.sqrt(ROWS * COLS / RANK)
    update = (update_scale * jnp.dot(left_basis, next_factor, precision=highest)).astype(jnp.bfloat16)
    return (next_momentum, update, next_factor)
```

```python
import itertools
import math

import jax
import jax.numpy as jnp
from jax import lax
from jax.experimental import pallas as pl
from jax.experimental.pallas import tpu as pltpu
from jax.sharding import PartitionSpec as P

ROWS = 8192
COLS = 27648
RANK = 256

decay_rate = 0.9
norm_eps = 1e-08

MESH = pl.DeviceIdType.MESH
HIGHEST = lax.Precision.HIGHEST
f32 = jnp.float32
bf16 = jnp.bfloat16

NX, NY, NZ = 4, 8, 12
LOCAL_ROWS = ROWS // 64
LOCAL = COLS // NZ
HALF = LOCAL // 2
CUT = 256
REST = HALF - CUT
CHUNK = 384
BLOCK = 16
OUTWARD = (1, 7, 2, 6, 3, 5, 4)
INWARD = (4, 3, 5, 2, 6, 1, 7)
COPIES = 384
VMEM_LIMIT = 48 << 20


def dot(a, b, dims, precision=HIGHEST):
    return lax.dot_general(a, b, (dims, ((), ())), precision=precision, preferred_element_type=f32)


def split3(a):
    first = a.astype(bf16)
    rest = a - first.astype(f32)
    second = rest.astype(bf16)
    third = (rest - second.astype(f32)).astype(bf16)
    return first, second, third


def factor_step(work, k):
    b, n = BLOCK, RANK
    first = pl.multiple_of(k * b, b)
    rows = work[pl.ds(first, b), :]
    lane = lax.broadcasted_iota(jnp.int32, (b, n), 1)
    row = lax.broadcasted_iota(jnp.int32, (b, n), 0)
    row128 = lax.broadcasted_iota(jnp.int32, (b, 128), 0)
    here = jnp.where(first >= 128, rows[:, 128:], rows[:, :128])
    here = pltpu.roll(here, lax.rem(128 - lax.rem(first, 128), 128), 1)
    column = [jnp.broadcast_to(here[:, j : j + 1], (b, 128)) for j in range(b)]
    inside = (lane >= first) & (lane < first + b)
    rows = jnp.where(inside, jnp.where(lane - first == row, 1.0, 0.0), rows)
    low, high = rows[:, :128], rows[:, 128:]
    pivots = jnp.ones((b, 128), f32)
    for j in range(b):
        pivot = column[j][j : j + 1, :]
        scaled = jnp.where(row128 > j, column[j] * (1.0 / pivot), 0.0)
        pivots = jnp.where(row128 == j, pivot, pivots)
        for i in range(j + 1, b):
            column[i] = column[i] - scaled * column[i][j : j + 1, :]
        low = low - scaled * low[j : j + 1, :]
        high = high - scaled * high[j : j + 1, :]
    scale = lax.rsqrt(pivots)
    rows = jnp.concatenate([low * scale, high * scale], axis=1)
    ahead = jnp.where(lane >= first + b, rows, 0.0)
    a1, a2, a3 = split3(ahead)
    r1, r2, r3 = split3(rows)
    change = dot(
        jnp.concatenate([a1, a1, a2, a2, a1, a3], axis=0),
        jnp.concatenate([r1, r2, r1, r2, r3, r1], axis=0),
        ((0,), (0,)),
        None,
    )
    lanes = lax.broadcasted_iota(jnp.int32, (n, n), 1)
    work[...] = jnp.where((lanes >= first) & (lanes < first + b), 0.0, work[...]) - change
    work[pl.ds(first, b), :] = rows


def kernel(
    mom, grad, rf, nm, up, nf,
    buf, rg, sib4, lp, zr, lf, gp, gs, gr, gsum, gr2, gg, mp, ms, ra, sa, ra2, rb, sb, rb2, mg, work, rr, sq, sqr,
    send, recv,
):
    f, z = lax.axis_index("fsdp"), lax.axis_index("tp")
    c, x, y = lax.rem(f, 2), lax.rem(lax.div(f, 2), NX), lax.div(f, 2 * NX)

    def wrap(v, n):
        return lax.rem(v + n, n)

    def at(dx=0, dy=0, dz=0, core=None):
        chip = wrap(y + dy, NY) * NX + wrap(x + dx, NX)
        return (chip * 2 + (c if core is None else core), wrap(z + dz, NZ))

    sibling = at(core=1 - c)
    number = itertools.count()
    started = []

    def go(src, dst, to):
        i = next(number)
        copy = pltpu.make_async_remote_copy(
            src_ref=src, dst_ref=dst, send_sem=send.at[i], recv_sem=recv.at[i], device_id=to, device_id_type=MESH
        )
        copy.start()
        started.append(copy)
        return copy

    peers = [sibling] + [at(dx=e) for e in range(1, NX)] + [at(dy=e) for e in range(1, NY)]
    peers += [at(dz=e) for e in range(1, NZ)]
    barrier = pltpu.get_barrier_semaphore()
    for peer in peers:
        pl.semaphore_signal(barrier, inc=1, device_id=peer, device_id_type=MESH)
    buf[...] = mom[...] + grad[...].astype(f32)
    pl.semaphore_wait(barrier, len(peers))

    class Gather:
        def __init__(self, ref):
            self.half = ref.at[c]
            self.cols_a, self.cols_b = pl.ds(0, CUT), pl.ds(CUT, REST)

        def start(self):
            half, a, b = self.half, self.cols_a, self.cols_b
            own_a, own_b = half.at[y, x, :, a], half.at[y, x, :, b]
            self.ax = [go(own_a, own_a, at(dx=e)) for e in range(1, NX)]
            self.by = {e: go(own_b, own_b, at(dy=e)) for e in OUTWARD}
            self.bx = {0: [go(own_b, own_b, at(dx=g)) for g in range(1, NX)]}

        def pass_a(self):
            for copy in self.ax:
                copy.wait_recv()
            line = self.half.at[y, :, :, self.cols_a]
            self.ay = [go(line, line, at(dy=e)) for e in INWARD]

        def pass_b(self, e):
            self.by[e].wait_recv()
            block = self.half.at[wrap(y - e, NY), x, :, self.cols_b]
            self.bx[e] = [go(block, block, at(dx=g)) for g in range(1, NX)]

        def hand_b(self, e):
            for copy in self.bx[e]:
                copy.wait_recv()
            line = self.half.at[wrap(y - e, NY), :, :, self.cols_b]
            self.given = getattr(self, "given", []) + [go(line, line, sibling)]

        def hand_a(self):
            for copy in self.ay:
                copy.wait_recv()
            part = self.half.at[:, :, :, self.cols_a]
            self.given.append(go(part, part, sibling))

        def finish(self):
            for copy in self.given:
                copy.wait_recv()

    other_cols = pl.ds(pl.multiple_of((1 - c) * HALF, 128), HALF)
    swap = go(rf.at[:, other_cols], sib4, sibling)
    swap.wait_recv()
    mine, theirs = rf[:, pl.ds(pl.multiple_of(c * HALF, 128), HALF)], sib4[...]
    rg[c, y, x, 0:4, :] = jnp.where(c == 0, mine, theirs)
    rg[c, y, x, 4:8, :] = jnp.where(c == 0, theirs, mine)
    gather = Gather(rg)
    gather.start()
    gather.pass_b(1)
    gather.pass_b(7)
    gather.pass_a()
    for e in OUTWARD[2:]:
        gather.pass_b(e)
    for e in (0,) + OUTWARD:
        gather.hand_b(e)
    gather.hand_a()

    def partial_left(core, total):
        def body(i, total):
            k = pl.multiple_of(i * CHUNK, 128)
            right = rg[core, :, :, :, pl.ds(k, CHUNK)].reshape(RANK, CHUNK)
            left = buf[:, pl.ds(pl.multiple_of(core * HALF + k, 128), CHUNK)]
            return total + dot(right, left, ((1,), (1,)))

        return lax.fori_loop(0, HALF // CHUNK, body, total)

    total = partial_left(c, jnp.zeros((RANK, LOCAL_ROWS), f32))
    gather.finish()
    total = partial_left(1 - c, total)

    lp[0:32] = total.reshape(32, 8, LOCAL_ROWS)
    lp[32:36] = jnp.zeros((4, 8, LOCAL_ROWS), f32)
    own_tiles = pl.ds(z * 3, 3)
    parts = []
    for e in range(1, NZ):
        parts.append(go(lp.at[pl.ds(wrap(z + e, NZ) * 3, 3)], zr.at[e - 1], at(dz=e)))
    for copy in parts:
        copy.wait_recv()
    tiles = lp[own_tiles]
    for e in range(1, NZ):
        tiles = tiles + zr[e - 1]
    lf[own_tiles] = tiles
    parts = [go(lf.at[own_tiles], lf.at[own_tiles], at(dz=e)) for e in range(1, NZ)]
    for copy in parts:
        copy.wait_recv()
    left = lf[0:32].reshape(RANK, LOCAL_ROWS)

    gram = dot(left, left, ((1,), (1,)))
    gp[0] = gram[:, :128].reshape(NY, NX, 8, 128)
    gp[1] = gram[:, 128:].reshape(NY, NX, 8, 128)
    gram_swap = go(gp.at[1 - c], gs, sibling)

    def partial_rows(core, k):
        cols = pl.ds(pl.multiple_of(core * HALF + k, 128), CHUNK)
        block = dot(left, buf[:, cols], ((1,), (0,)))
        mp[core, :, :, :, pl.ds(k, CHUNK)] = block.reshape(NY, NX, 8, CHUNK)

    rows_swap = []
    for k in range(0, HALF, CHUNK):
        partial_rows(1 - c, k)
        cols = pl.ds(k, CHUNK)
        rows_swap.append(go(mp.at[1 - c, :, :, :, cols], ms.at[:, :, :, cols], sibling))
    gram_swap.wait_recv()
    gs[...] = gs[...] + gp[c]
    gram_y = [go(gs.at[wrap(y + e, NY)], gr.at[e - 1], at(dy=e)) for e in INWARD]
    for k in range(0, HALF, CHUNK):
        partial_rows(c, k)
    for i, k in enumerate(range(0, HALF, CHUNK)):
        rows_swap[i].wait_recv()
        cols = pl.ds(k, CHUNK)
        ms[:, :, :, cols] = ms[:, :, :, cols] + mp[c, :, :, :, cols]

    cols_a, cols_b = pl.ds(0, CUT), pl.ds(CUT, REST)
    scatter_a = [go(ms.at[wrap(y + e, NY), :, :, cols_a], ra.at[e - 1], at(dy=e)) for e in INWARD]
    scatter_b = {}
    for e in INWARD + (0,):
        row = wrap(y + e, NY)
        scatter_b[e] = [
            go(ms.at[row, wrap(x + g, NX), :, cols_b], rb.at[e, g - 1], at(dx=g)) for g in range(1, NX)
        ]

    def gram_sum_y():
        for copy in gram_y:
            copy.wait_recv()
        part = gs[y]
        for e in range(1, NY):
            part = part + gr[e - 1]
        gsum[...] = part
        return [go(gsum.at[wrap(x + g, NX)], gr2.at[g - 1], at(dx=g)) for g in range(1, NX)]

    def gram_sum_x(copies):
        for copy in copies:
            copy.wait_recv()
        part = gsum[x]
        for g in range(1, NX):
            part = part + gr2[g - 1]
        gg[c, y, x] = part
        own = gg.at[c, y, x]
        return [go(own, own, at(dx=g)) for g in range(1, NX)]

    def gram_spread_y(copies):
        for copy in copies:
            copy.wait_recv()
        line = gg.at[c, y]
        return [go(line, line, at(dy=e)) for e in INWARD]

    def gram_hand(copies):
        for copy in copies:
            copy.wait_recv()
        return go(gg.at[c], gg.at[c], sibling)

    def sum_b(e):
        for copy in scatter_b[e]:
            copy.wait_recv()
        part = ms[wrap(y + e, NY), x, :, cols_b]
        for g in range(1, NX):
            part = part + rb[e, g - 1]
        return part

    second_b = []

    def relay_b(e):
        sb[e - 1] = sum_b(e)
        second_b.append(go(sb.at[e - 1], rb2.at[e - 1], at(dy=e)))

    gram_copies = gram_sum_y()
    for e in INWARD[:3]:
        relay_b(e)
    gram_copies = gram_sum_x(gram_copies)
    for e in INWARD[3:5]:
        relay_b(e)
    gram_copies = gram_spread_y(gram_copies)
    for e in INWARD[5:]:
        relay_b(e)
    for copy in scatter_a:
        copy.wait_recv()
    part = ms[y, :, :, cols_a]
    for e in range(1, NY):
        part = part + ra[e - 1]
    sa[...] = part
    second_a = [go(sa.at[wrap(x + g, NX)], ra2.at[g - 1], at(dx=g)) for g in range(1, NX)]
    part_b = sum_b(0)
    gram_copy = gram_hand(gram_copies)
    for copy in second_b:
        copy.wait_recv()
    for e in range(1, NY):
        part_b = part_b + rb2[e - 1]
    mg[c, y, x, :, cols_b] = part_b
    for copy in second_a:
        copy.wait_recv()
    part = sa[x]
    for g in range(1, NX):
        part = part + ra2[g - 1]
    mg[c, y, x, :, cols_a] = part

    gather = Gather(mg)
    gather.start()
    gram_copy.wait_recv()
    work[:, :128] = gg[0].reshape(RANK, 128)
    work[:, 128:] = gg[1].reshape(RANK, 128)

    def factor(first, last):
        def body(k, carry):
            factor_step(work, k)
            return carry

        lax.fori_loop(first, last, body, 0)

    factor(0, 5)
    gather.pass_b(1)
    gather.pass_b(7)
    factor(5, 7)
    gather.pass_a()
    gather.pass_b(2)
    gather.pass_b(6)
    factor(7, 9)
    gather.pass_b(3)
    gather.pass_b(5)
    factor(9, 11)
    gather.pass_b(4)
    gather.hand_b(0)
    factor(11, 13)
    gather.hand_b(1)
    gather.hand_b(7)
    factor(13, 15)
    gather.hand_b(2)
    gather.hand_b(6)
    factor(15, 16)
    r = lax.broadcasted_iota(jnp.int32, (RANK, RANK), 0)
    l = lax.broadcasted_iota(jnp.int32, (RANK, RANK), 1)
    inverse = jnp.where(l <= r, work[...], 0.0)
    work[...] = inverse
    basis = dot(left, inverse, ((0,), (1,)))
    for e in OUTWARD[4:]:
        gather.hand_b(e)
    gather.hand_a()

    def right_rows(core, squares):
        def body(i, squares):
            k = pl.multiple_of(i * CHUNK, 128)
            block = dot(work[...], mg[core, :, :, :, pl.ds(k, CHUNK)].reshape(RANK, CHUNK), ((1,), (0,)))
            rr[:, pl.ds(pl.multiple_of(core * HALF + k, 128), CHUNK)] = block
            for t in range(0, CHUNK, 128):
                squares = squares + block[:, t : t + 128] * block[:, t : t + 128]
            return squares

        return lax.fori_loop(0, HALF // CHUNK, body, squares)

    squares = right_rows(c, jnp.zeros((RANK, 128), f32))
    gather.finish()
    squares = right_rows(1 - c, squares)
    sq[...] = dot(jnp.ones((8, 128), f32), squares, ((1,), (1,)))
    parts = [go(sq, sqr.at[e - 1], at(dz=e)) for e in range(1, NZ)]

    basis16 = basis.astype(bf16)

    def momentum_body(i, carry):
        cols = pl.ds(pl.multiple_of(i * CHUNK, 128), CHUNK)
        product = dot(basis16, rr[:, cols].astype(bf16), ((1,), (0,)), None)
        nm[:, cols] = buf[:, cols] - (1.0 - decay_rate) * product
        return carry

    lax.fori_loop(0, LOCAL // CHUNK, momentum_body, 0)
    for copy in parts:
        copy.wait_recv()
    norm = sq[...]
    for e in range(1, NZ):
        norm = norm + sqr[e - 1]
    inverse_norm = 1.0 / (jnp.sqrt(norm) + norm_eps)
    scaled = basis * (math.sqrt(ROWS * COLS / RANK) * inverse_norm[0:1, :])
    s1 = scaled.astype(bf16)
    s2 = (scaled - s1.astype(f32)).astype(bf16)

    def update_body(i, carry):
        cols = pl.ds(pl.multiple_of(i * CHUNK, 128), CHUNK)
        block = rr[:, cols]
        b1 = block.astype(bf16)
        b2 = (block - b1.astype(f32)).astype(bf16)
        dims = ((1,), (0,))
        product = dot(s1, b1, dims, None) + (dot(s1, b2, dims, None) + dot(s2, b1, dims, None))
        up[:, cols] = product.astype(bf16)
        return carry

    lax.fori_loop(0, LOCAL // CHUNK, update_body, 0)
    chip = y * NX + x
    eight = rr[pl.ds(pl.multiple_of(chip * 8, 8), 8), :]
    r = lax.broadcasted_iota(jnp.int32, (8, RANK), 0)
    l = lax.broadcasted_iota(jnp.int32, (8, RANK), 1)
    own = jnp.sum(jnp.where(l == r + chip * 8, inverse_norm, 0.0), axis=1, keepdims=True)
    eight = eight * own
    nf[...] = jnp.where(c == 0, eight[0:4, :], eight[4:8, :])

    for copy in started:
        copy.wait_send()


def shards(momentum, gradient, right_factor):
    vmem = pl.BlockSpec(memory_space=pltpu.VMEM)
    scratch = [
        (LOCAL_ROWS, LOCAL),
        (2, NY, NX, 8, HALF),
        (4, HALF),
        (36, 8, LOCAL_ROWS),
        (NZ - 1, 3, 8, LOCAL_ROWS),
        (36, 8, LOCAL_ROWS),
        (2, NY, NX, 8, 128),
        (NY, NX, 8, 128),
        (NY - 1, NX, 8, 128),
        (NX, 8, 128),
        (NX - 1, 8, 128),
        (2, NY, NX, 8, 128),
        (2, NY, NX, 8, HALF),
        (NY, NX, 8, HALF),
        (NY - 1, NX, 8, CUT),
        (NX, 8, CUT),
        (NX - 1, 8, CUT),
        (NY, NX - 1, 8, REST),
        (NY - 1, 8, REST),
        (NY - 1, 8, REST),
        (2, NY, NX, 8, HALF),
        (RANK, RANK),
        (RANK, LOCAL),
        (8, RANK),
        (NZ - 1, 8, RANK),
    ]
    return pl.pallas_call(
        kernel,
        out_shape=(
            jax.ShapeDtypeStruct((LOCAL_ROWS, LOCAL), f32),
            jax.ShapeDtypeStruct((LOCAL_ROWS, LOCAL), bf16),
            jax.ShapeDtypeStruct((4, LOCAL), f32),
        ),
        in_specs=[vmem] * 3,
        out_specs=(vmem,) * 3,
        scratch_shapes=[pltpu.VMEM(shape, f32) for shape in scratch]
        + [pltpu.SemaphoreType.DMA((COPIES,)), pltpu.SemaphoreType.DMA((COPIES,))],
        compiler_params=pltpu.CompilerParams(collective_id=0, has_side_effects=True, vmem_limit_bytes=VMEM_LIMIT),
    )(momentum, gradient, right_factor)


def solution(mesh):
    spec = P("fsdp", "tp")
    return jax.shard_map(shards, mesh=mesh, in_specs=(spec,) * 3, out_specs=(spec,) * 3, check_vma=False)
```

```python
import itertools
import math

import jax
import jax.numpy as jnp
from jax import lax
from jax.experimental import pallas as pl
from jax.experimental.pallas import tpu as pltpu
from jax.sharding import PartitionSpec as P

ROWS = 8192
COLS = 27648
RANK = 256

decay_rate = 0.9
norm_eps = 1e-08

MESH = pl.DeviceIdType.MESH
HIGHEST = lax.Precision.HIGHEST
f32 = jnp.float32
bf16 = jnp.bfloat16

NX, NY, NZ = 4, 8, 12
LOCAL_ROWS = ROWS // 64
LOCAL = COLS // NZ
HALF = LOCAL // 2
CUT = 256
REST = HALF - CUT
PART = 384
CHUNK = 384
WIDE = 768
BLOCK = 16
OUTWARD = (1, 7, 2, 6, 3, 5, 4)
INWARD = (4, 3, 5, 2, 6, 1, 7)
COPIES = 384
VMEM_LIMIT = 32 << 20


def dot(a, b, dims, precision=HIGHEST):
    return lax.dot_general(a, b, (dims, ((), ())), precision=precision, preferred_element_type=f32)


def split3(a):
    first = a.astype(bf16)
    rest = a - first.astype(f32)
    second = rest.astype(bf16)
    third = (rest - second.astype(f32)).astype(bf16)
    return first, second, third


def factor_step(work, k):
    b, n = BLOCK, RANK
    first = pl.multiple_of(k * b, b)
    rows = work[pl.ds(first, b), :]
    lane = lax.broadcasted_iota(jnp.int32, (b, n), 1)
    row = lax.broadcasted_iota(jnp.int32, (b, n), 0)
    row128 = lax.broadcasted_iota(jnp.int32, (b, 128), 0)
    here = jnp.where(first >= 128, rows[:, 128:], rows[:, :128])
    here = pltpu.roll(here, lax.rem(128 - lax.rem(first, 128), 128), 1)
    column = [jnp.broadcast_to(here[:, j : j + 1], (b, 128)) for j in range(b)]
    inside = (lane >= first) & (lane < first + b)
    rows = jnp.where(inside, jnp.where(lane - first == row, 1.0, 0.0), rows)
    low, high = rows[:, :128], rows[:, 128:]
    pivots = jnp.ones((b, 128), f32)
    for j in range(b):
        pivot = column[j][j : j + 1, :]
        scaled = jnp.where(row128 > j, column[j] * (1.0 / pivot), 0.0)
        pivots = jnp.where(row128 == j, pivot, pivots)
        for i in range(j + 1, b):
            column[i] = column[i] - scaled * column[i][j : j + 1, :]
        low = low - scaled * low[j : j + 1, :]
        high = high - scaled * high[j : j + 1, :]
    scale = lax.rsqrt(pivots)
    rows = jnp.concatenate([low * scale, high * scale], axis=1)
    ahead = jnp.where(lane >= first + b, rows, 0.0)
    a1, a2, a3 = split3(ahead)
    r1, r2, r3 = split3(rows)
    change = dot(
        jnp.concatenate([a1, a1, a2, a2, a1, a3], axis=0),
        jnp.concatenate([r1, r2, r1, r2, r3, r1], axis=0),
        ((0,), (0,)),
        None,
    )
    lanes = lax.broadcasted_iota(jnp.int32, (n, n), 1)
    work[...] = jnp.where((lanes >= first) & (lanes < first + b), 0.0, work[...]) - change
    work[pl.ds(first, b), :] = rows


def kernel(
    mom_hbm, grad_hbm, rf_hbm, nm, rr, scaled_ref, nf,
    mom, rf, buf, rg, sib4, lp, zr, lf, gp, gs, gr, gsum, gr2, gg, mp, ms, ra, ra1, sa, ra2, rb, sb, rb2, rb4, mg, work, sq, sqr,
    grad, send, recv, load,
):
    f, z = lax.axis_index("fsdp"), lax.axis_index("tp")
    c, x, y = lax.rem(f, 2), lax.rem(lax.div(f, 2), NX), lax.div(f, 2 * NX)

    def wrap(v, n):
        return lax.rem(v + n, n)

    def at(dx=0, dy=0, dz=0, core=None):
        chip = wrap(y + dy, NY) * NX + wrap(x + dx, NX)
        return (chip * 2 + (c if core is None else core), wrap(z + dz, NZ))

    sibling = at(core=1 - c)
    number = itertools.count()
    started = []

    def go(src, dst, to):
        i = next(number)
        copy = pltpu.make_async_remote_copy(
            src_ref=src, dst_ref=dst, send_sem=send.at[i], recv_sem=recv.at[i], device_id=to, device_id_type=MESH
        )
        copy.start()
        started.append(copy)
        return copy

    loads = [
        pltpu.make_async_copy(src, dst, load.at[i])
        for i, (src, dst) in enumerate(((rf_hbm, rf), (mom_hbm, mom), (grad_hbm, grad)))
    ]
    for copy in loads:
        copy.start()
    peers = [sibling] + [at(dx=e) for e in range(1, NX)] + [at(dy=e) for e in range(1, NY)]
    peers += [at(dz=e) for e in range(1, NZ)]
    barrier = pltpu.get_barrier_semaphore()
    for peer in peers:
        pl.semaphore_signal(barrier, inc=1, device_id=peer, device_id_type=MESH)
    loads[0].wait()
    pl.semaphore_wait(barrier, len(peers))

    class Gather:
        def __init__(self, ref):
            self.half = ref.at[c]
            self.cols_a, self.cols_b = pl.ds(0, CUT), pl.ds(CUT, REST)

        def start(self):
            half, a, b = self.half, self.cols_a, self.cols_b
            own_a, own_b = half.at[y, x, :, a], half.at[y, x, :, b]
            self.ax = [go(own_a, own_a, at(dx=e)) for e in range(1, NX)]
            self.by = {e: go(own_b, own_b, at(dy=e)) for e in OUTWARD}
            self.bx = {0: [go(own_b, own_b, at(dx=g)) for g in range(1, NX)]}

        def pass_a(self):
            for copy in self.ax:
                copy.wait_recv()
            line = self.half.at[y, :, :, self.cols_a]
            self.ay = [go(line, line, at(dy=e)) for e in INWARD]

        def pass_b(self, e):
            self.by[e].wait_recv()
            block = self.half.at[wrap(y - e, NY), x, :, self.cols_b]
            self.bx[e] = [go(block, block, at(dx=g)) for g in range(1, NX)]

        def hand_b(self, e):
            for copy in self.bx[e]:
                copy.wait_recv()
            line = self.half.at[wrap(y - e, NY), :, :, self.cols_b]
            self.given = getattr(self, "given", []) + [go(line, line, sibling)]

        def hand_a(self):
            for copy in self.ay:
                copy.wait_recv()
            part = self.half.at[:, :, :, self.cols_a]
            self.given.append(go(part, part, sibling))

        def finish(self):
            for copy in self.given:
                copy.wait_recv()

    other_cols = pl.ds(pl.multiple_of((1 - c) * HALF, 128), HALF)
    swap = go(rf.at[:, other_cols], sib4, sibling)
    swap.wait_recv()
    mine, theirs = rf[:, pl.ds(pl.multiple_of(c * HALF, 128), HALF)], sib4[...]
    rg[c, y, x, 0:4, :] = jnp.where(c == 0, mine, theirs)
    rg[c, y, x, 4:8, :] = jnp.where(c == 0, theirs, mine)
    gather = Gather(rg)
    gather.start()
    for copy in loads[1:]:
        copy.wait()
    buf[...] = mom[...] + grad[...].astype(f32)
    for e in OUTWARD[:4]:
        gather.pass_b(e)
    gather.pass_a()
    for e in OUTWARD[4:]:
        gather.pass_b(e)
    for e in (0,) + OUTWARD:
        gather.hand_b(e)
    gather.hand_a()

    def partial_left(core, total):
        def body(i, total):
            k = pl.multiple_of(i * CHUNK, 128)
            right = rg[core, :, :, :, pl.ds(k, CHUNK)].reshape(RANK, CHUNK)
            left = buf[:, pl.ds(pl.multiple_of(core * HALF + k, 128), CHUNK)]
            return total + dot(right, left, ((1,), (1,)))

        return lax.fori_loop(0, HALF // CHUNK, body, total)

    total = partial_left(c, jnp.zeros((RANK, LOCAL_ROWS), f32))
    gather.finish()
    total = partial_left(1 - c, total)

    lp[0:32] = total.reshape(32, 8, LOCAL_ROWS)
    lp[32:36] = jnp.zeros((4, 8, LOCAL_ROWS), f32)
    own_tiles = pl.ds(z * 3, 3)
    parts = []
    for e in range(1, NZ):
        parts.append(go(lp.at[pl.ds(wrap(z + e, NZ) * 3, 3)], zr.at[e - 1], at(dz=e)))
    for copy in parts:
        copy.wait_recv()
    tiles = lp[own_tiles]
    for e in range(1, NZ):
        tiles = tiles + zr[e - 1]
    lf[own_tiles] = tiles
    parts = [go(lf.at[own_tiles], lf.at[own_tiles], at(dz=e)) for e in range(1, NZ)]
    for copy in parts:
        copy.wait_recv()
    left = lf[0:32].reshape(RANK, LOCAL_ROWS)

    gram = dot(left, left, ((1,), (1,)))
    gp[0] = gram[:, :128].reshape(NY, NX, 8, 128)
    gp[1] = gram[:, 128:].reshape(NY, NX, 8, 128)
    gram_swap = go(gp.at[1 - c], gs, sibling)

    def partial_rows(core, k):
        cols = pl.ds(pl.multiple_of(core * HALF + k, 128), CHUNK)
        block = dot(left, buf[:, cols], ((1,), (0,)))
        mp[core, :, :, :, pl.ds(k, CHUNK)] = block.reshape(NY, NX, 8, CHUNK)

    rows_swap = []
    for k in range(0, HALF, CHUNK):
        partial_rows(1 - c, k)
        cols = pl.ds(k, CHUNK)
        rows_swap.append(go(mp.at[1 - c, :, :, :, cols], ms.at[:, :, :, cols], sibling))
    gram_swap.wait_recv()
    gs[...] = gs[...] + gp[c]
    gram_x = [go(gs.at[:, wrap(x + g, NX)], gr.at[g - 1], at(dx=g)) for g in (2, 1, 3)]
    for k in range(0, HALF, CHUNK):
        partial_rows(c, k)
    for i, k in enumerate(range(0, HALF, CHUNK)):
        rows_swap[i].wait_recv()
        cols = pl.ds(k, CHUNK)
        ms[:, :, :, cols] = ms[:, :, :, cols] + mp[c, :, :, :, cols]

    cols_a, cols_b = pl.ds(0, CUT), pl.ds(CUT, REST)
    low, high = pl.ds(CUT, PART), pl.ds(CUT + PART, REST - PART)

    def line_a(e, first=0, count=NX):
        return ms.at[wrap(y + e, NY), pl.ds(first, count), :, cols_a]

    def block_b(e, dx):
        return ms.at[wrap(y + e, NY), wrap(x + dx, NX), :, cols_b]

    near_a = [
        go(line_a(3), ra1.at[0], at(dy=1)),
        go(line_a(5), ra1.at[1], at(dy=-1)),
        go(line_a(4, 0, 2), ra1.at[2, pl.ds(0, 2)], at(dy=2)),
        go(line_a(4, 2, 2), ra1.at[3, pl.ds(2, 2)], at(dy=-2)),
    ]
    order = (4, 3, 5, 2, 6, 1, 7, 0)
    first_b, direct_b, relay_b = {}, {}, {}
    for e in order:
        step = 1 if e % 2 == 0 else -1
        first_b[e] = go(block_b(e, 2), rb.at[e, 0], at(dx=step))
        direct_b[e] = go(block_b(e, -step), rb.at[e, 1], at(dx=-step))
    far_a = {e: go(line_a(e), ra.at[e - 1], at(dy=e)) for e in (1, 7)}

    def relay_x(e):
        step = 1 if e % 2 == 0 else -1
        first_b[e].wait_recv()
        block = block_b(e, step)
        block[...] = block[...] + rb[e, 0]
        relay_b[e] = go(block, rb.at[e, 2], at(dx=step))

    def relay_a():
        for copy in near_a:
            copy.wait_recv()
        forward, back = wrap(y + 2, NY), wrap(y - 2, NY)
        ms[forward, :, :, cols_a] = ms[forward, :, :, cols_a] + ra1[0]
        ms[forward, 0:2, :, cols_a] = ms[forward, 0:2, :, cols_a] + ra1[2, 0:2]
        ms[back, :, :, cols_a] = ms[back, :, :, cols_a] + ra1[1]
        ms[back, 2:4, :, cols_a] = ms[back, 2:4, :, cols_a] + ra1[3, 2:4]
        far_a.update({e: go(line_a(e), ra.at[e - 1], at(dy=e)) for e in (2, 6)})

    def sum_a():
        for e in (1, 7, 2, 6):
            far_a[e].wait_recv()
        sa[...] = ms[y, :, :, cols_a] + ra[0] + ra[6] + ra[1] + ra[5]
        return [go(sa.at[wrap(x + g, NX)], ra2.at[g - 1], at(dx=g)) for g in (2, 1, 3)]

    def sum_b(e):
        direct_b[e].wait_recv()
        relay_b[e].wait_recv()
        return ms[wrap(y + e, NY), x, :, cols_b] + rb[e, 1] + rb[e, 2]

    last_b, quarter = [], []

    def send_y(e):
        sb[e] = sum_b(e)
        if e == 4:
            for part, way in ((pl.ds(0, PART), 2), (pl.ds(PART, REST - PART), -2)):
                quarter.append(go(sb.at[4, :, part], rb4.at[:, part], at(dy=way)))
        else:
            last_b.append(go(sb.at[e], rb2.at[e - 1], at(dy=e)))

    def send_two():
        for copy in quarter:
            copy.wait_recv()
        total = sum_b(2)
        sb[2, :, :PART] = total[:, :PART] + rb4[:, :PART]
        sb[2, :, PART:] = total[:, PART:]
        last_b.append(go(sb.at[2], rb2.at[1], at(dy=2)))
        total = sum_b(6)
        sb[6, :, :PART] = total[:, :PART]
        sb[6, :, PART:] = total[:, PART:] + rb4[:, PART:]
        last_b.append(go(sb.at[6], rb2.at[5], at(dy=6)))

    def gram_sum_x():
        for copy in gram_x:
            copy.wait_recv()
        part = gs[:, x]
        for g in range(1, NX):
            part = part + gr[g - 1]
        gsum[...] = part
        return [go(gsum.at[wrap(y + e, NY)], gr2.at[e - 1], at(dy=e)) for e in INWARD]

    def gram_sum_y(copies):
        for copy in copies:
            copy.wait_recv()
        part = gsum[y]
        for e in range(1, NY):
            part = part + gr2[e - 1]
        gg[c, y, x] = part
        own = gg.at[c, y, x]
        return [go(own, own, at(dy=e)) for e in INWARD]

    def gram_spread_x(copies):
        for copy in copies:
            copy.wait_recv()
        line = gg.at[c, :, x]
        return [go(line, line, at(dx=g)) for g in (2, 1, 3)]

    def gram_hand(copies):
        for copy in copies:
            copy.wait_recv()
        return go(gg.at[c], gg.at[c], sibling)

    gram_copies = gram_sum_x()
    for e in order[:5]:
        relay_x(e)
    relay_a()
    gram_copies = gram_sum_y(gram_copies)
    for e in order[5:]:
        relay_x(e)
    for e in (4, 3, 5):
        send_y(e)
    gram_copies = gram_spread_x(gram_copies)
    for e in (1, 7):
        send_y(e)
    second_a = sum_a()
    send_two()
    part_b = sum_b(0)
    for copy in second_a:
        copy.wait_recv()
    part = sa[x]
    for g in range(1, NX):
        part = part + ra2[g - 1]
    mg[c, y, x, :, cols_a] = part
    for copy in last_b:
        copy.wait_recv()
    for e in (1, 7, 2, 6, 3, 5):
        part_b = part_b + rb2[e - 1]
    mg[c, y, x, :, cols_b] = part_b

    gather = Gather(mg)
    gather.start()
    gram_copy = gram_hand(gram_copies)
    for e in OUTWARD[:4]:
        gather.pass_b(e)
    gather.pass_a()
    gram_copy.wait_recv()
    work[:, :128] = gg[0].reshape(RANK, 128)
    work[:, 128:] = gg[1].reshape(RANK, 128)

    def factor(first, last):
        def body(k, carry):
            factor_step(work, k)
            return carry

        lax.fori_loop(first, last, body, 0)

    factor(0, 1)
    gather.pass_b(3)
    gather.pass_b(5)
    factor(1, 2)
    gather.pass_b(4)
    factor(2, 6)
    gather.hand_b(0)
    factor(6, 8)
    gather.hand_b(1)
    gather.hand_b(7)
    factor(8, 10)
    gather.hand_b(2)
    gather.hand_b(6)
    factor(10, 13)
    gather.hand_b(3)
    gather.hand_b(5)
    factor(13, 15)
    gather.hand_b(4)
    gather.hand_a()
    factor(15, 16)
    r = lax.broadcasted_iota(jnp.int32, (RANK, RANK), 0)
    l = lax.broadcasted_iota(jnp.int32, (RANK, RANK), 1)
    inverse = jnp.where(l <= r, work[...], 0.0)
    work[...] = inverse
    basis = dot(left, inverse, ((0,), (1,)))

    def right_rows(core, squares):
        def body(i, squares):
            k = pl.multiple_of(i * CHUNK, 128)
            block = dot(work[...], mg[core, :, :, :, pl.ds(k, CHUNK)].reshape(RANK, CHUNK), ((1,), (0,)))
            rr[:, pl.ds(pl.multiple_of(core * HALF + k, 128), CHUNK)] = block
            for t in range(0, CHUNK, 128):
                squares = squares + block[:, t : t + 128] * block[:, t : t + 128]
            return squares

        return lax.fori_loop(0, HALF // CHUNK, body, squares)

    squares = right_rows(c, jnp.zeros((RANK, 128), f32))
    gather.finish()
    squares = right_rows(1 - c, squares)
    sq[...] = dot(jnp.ones((8, 128), f32), squares, ((1,), (1,)))
    parts = [go(sq, sqr.at[e - 1], at(dz=e)) for e in range(1, NZ)]

    basis16 = basis.astype(bf16)

    def momentum_body(i, carry):
        cols = pl.ds(pl.multiple_of(i * CHUNK, 128), CHUNK)
        product = dot(basis16, rr[:, cols].astype(bf16), ((1,), (0,)), None)
        nm[:, cols] = buf[:, cols] - (1.0 - decay_rate) * product
        return carry

    lax.fori_loop(0, LOCAL // CHUNK, momentum_body, 0)
    for copy in parts:
        copy.wait_recv()
    norm = sq[...]
    for e in range(1, NZ):
        norm = norm + sqr[e - 1]
    inverse_norm = 1.0 / (jnp.sqrt(norm) + norm_eps)
    scaled = basis * (math.sqrt(ROWS * COLS / RANK) * inverse_norm[0:1, :])
    scaled_ref[...] = scaled
    chip = y * NX + x
    eight = rr[pl.ds(pl.multiple_of(chip * 8, 8), 8), :]
    r = lax.broadcasted_iota(jnp.int32, (8, RANK), 0)
    l = lax.broadcasted_iota(jnp.int32, (8, RANK), 1)
    own = jnp.sum(jnp.where(l == r + chip * 8, inverse_norm, 0.0), axis=1, keepdims=True)
    eight = eight * own
    nf[...] = jnp.where(c == 0, eight[0:4, :], eight[4:8, :])

    for copy in started:
        copy.wait_send()


def finish(nm, rr, scaled, nf, nm_out, up_out, nf_out, up, done):
    copies = [pltpu.make_async_copy(nm, nm_out, done.at[0]), pltpu.make_async_copy(nf, nf_out, done.at[1])]
    for copy in copies:
        copy.start()
    s = scaled[...]
    s1 = s.astype(bf16)
    s2 = (s - s1.astype(f32)).astype(bf16)
    for i in range(LOCAL // WIDE):
        cols = pl.ds(i * WIDE, WIDE)
        block = rr[:, cols]
        b1 = block.astype(bf16)
        b2 = (block - b1.astype(f32)).astype(bf16)
        dims = ((1,), (0,))
        product = dot(s1, b1, dims, None) + (dot(s1, b2, dims, None) + dot(s2, b1, dims, None))
        up[:, cols] = product.astype(bf16)
        copies.append(pltpu.make_async_copy(up.at[:, cols], up_out.at[:, cols], done.at[2 + i]))
        copies[-1].start()
    for copy in copies:
        copy.wait()


def shards(momentum, gradient, right_factor):
    vmem = pl.BlockSpec(memory_space=pltpu.VMEM)
    hbm = pl.BlockSpec(memory_space=pltpu.HBM)
    scratch = [
        (LOCAL_ROWS, LOCAL),
        (4, LOCAL),
        (LOCAL_ROWS, LOCAL),
        (2, NY, NX, 8, HALF),
        (4, HALF),
        (36, 8, LOCAL_ROWS),
        (NZ - 1, 3, 8, LOCAL_ROWS),
        (36, 8, LOCAL_ROWS),
        (2, NY, NX, 8, 128),
        (NY, NX, 8, 128),
        (NX - 1, NY, 8, 128),
        (NY, 8, 128),
        (NY - 1, 8, 128),
        (2, NY, NX, 8, 128),
        (2, NY, NX, 8, HALF),
        (NY, NX, 8, HALF),
        (NY - 1, NX, 8, CUT),
        (4, NX, 8, CUT),
        (NX, 8, CUT),
        (NX - 1, 8, CUT),
        (NY, 3, 8, REST),
        (NY, 8, REST),
        (NY - 1, 8, REST),
        (8, REST),
        (2, NY, NX, 8, HALF),
        (RANK, RANK),
        (8, RANK),
        (NZ - 1, 8, RANK),
    ]
    shape = jax.ShapeDtypeStruct
    parts = pl.pallas_call(
        kernel,
        out_shape=(
            shape((LOCAL_ROWS, LOCAL), f32),
            shape((RANK, LOCAL), f32),
            shape((LOCAL_ROWS, RANK), f32),
            shape((4, LOCAL), f32),
        ),
        in_specs=[hbm] * 3,
        out_specs=(vmem,) * 4,
        scratch_shapes=[pltpu.VMEM(each, f32) for each in scratch]
        + [pltpu.VMEM((LOCAL_ROWS, LOCAL), bf16)]
        + [pltpu.SemaphoreType.DMA((COPIES,)), pltpu.SemaphoreType.DMA((COPIES,)), pltpu.SemaphoreType.DMA((3,))],
        compiler_params=pltpu.CompilerParams(collective_id=0, has_side_effects=True, vmem_limit_bytes=VMEM_LIMIT),
    )(*[pltpu.with_memory_space_constraint(a, pltpu.HBM) for a in (momentum, gradient, right_factor)])
    return pl.pallas_call(
        finish,
        out_shape=(
            shape((LOCAL_ROWS, LOCAL), f32),
            shape((LOCAL_ROWS, LOCAL), bf16),
            shape((4, LOCAL), f32),
        ),
        in_specs=[vmem] * 4,
        out_specs=(hbm,) * 3,
        scratch_shapes=[pltpu.VMEM((LOCAL_ROWS, LOCAL), bf16), pltpu.SemaphoreType.DMA((2 + LOCAL // WIDE,))],
        compiler_params=pltpu.CompilerParams(vmem_limit_bytes=16 << 20),
    )(*parts)


def solution(mesh):
    spec = P("fsdp", "tp")
    return jax.shard_map(shards, mesh=mesh, in_specs=(spec,) * 3, out_specs=(spec,) * 3, check_vma=False)
```

```python
import itertools
import math

import jax
import jax.numpy as jnp
from jax import lax
from jax.experimental import pallas as pl
from jax.experimental.pallas import tpu as pltpu
from jax.sharding import PartitionSpec as P

ROWS = 8192
COLS = 27648
RANK = 256

decay_rate = 0.9
norm_eps = 1e-08

MESH = pl.DeviceIdType.MESH
HIGHEST = lax.Precision.HIGHEST
f32 = jnp.float32
bf16 = jnp.bfloat16

NX, NY, NZ = 4, 8, 12
LOCAL_ROWS = ROWS // 64
LOCAL = COLS // NZ
HALF = LOCAL // 2
CUT = 256
REST = HALF - CUT
PART = 384
CHUNK = 384
WIDE = 768
BLOCK = 16
OUTWARD = (1, 7, 2, 6, 3, 5, 4)
INWARD = (4, 3, 5, 2, 6, 1, 7)
AROUND = (6, 5, 7, 4, 8, 3, 9, 2, 10, 1, 11)
COPIES = 384
VMEM_LIMIT = 32 << 20


def dot(a, b, dims, precision=HIGHEST):
    return lax.dot_general(a, b, (dims, ((), ())), precision=precision, preferred_element_type=f32)


def split3(a):
    first = a.astype(bf16)
    rest = a - first.astype(f32)
    second = rest.astype(bf16)
    third = (rest - second.astype(f32)).astype(bf16)
    return first, second, third


def factor_step(work, k):
    b, n = BLOCK, RANK
    first = pl.multiple_of(k * b, b)
    rows = work[pl.ds(first, b), :]
    lane = lax.broadcasted_iota(jnp.int32, (b, n), 1)
    row = lax.broadcasted_iota(jnp.int32, (b, n), 0)
    row128 = lax.broadcasted_iota(jnp.int32, (b, 128), 0)
    here = jnp.where(first >= 128, rows[:, 128:], rows[:, :128])
    here = pltpu.roll(here, lax.rem(128 - lax.rem(first, 128), 128), 1)
    column = [jnp.broadcast_to(here[:, j : j + 1], (b, 128)) for j in range(b)]
    inside = (lane >= first) & (lane < first + b)
    rows = jnp.where(inside, jnp.where(lane - first == row, 1.0, 0.0), rows)
    low, high = rows[:, :128], rows[:, 128:]
    pivots = jnp.ones((b, 128), f32)
    for j in range(b):
        pivot = column[j][j : j + 1, :]
        scaled = jnp.where(row128 > j, column[j] * (1.0 / pivot), 0.0)
        pivots = jnp.where(row128 == j, pivot, pivots)
        for i in range(j + 1, b):
            column[i] = column[i] - scaled * column[i][j : j + 1, :]
        low = low - scaled * low[j : j + 1, :]
        high = high - scaled * high[j : j + 1, :]
    scale = lax.rsqrt(pivots)
    rows = jnp.concatenate([low * scale, high * scale], axis=1)
    ahead = jnp.where(lane >= first + b, rows, 0.0)
    a1, a2, a3 = split3(ahead)
    r1, r2, r3 = split3(rows)
    change = dot(
        jnp.concatenate([a1, a1, a2, a2, a1, a3], axis=0),
        jnp.concatenate([r1, r2, r1, r2, r3, r1], axis=0),
        ((0,), (0,)),
        None,
    )
    lanes = lax.broadcasted_iota(jnp.int32, (n, n), 1)
    work[...] = jnp.where((lanes >= first) & (lanes < first + b), 0.0, work[...]) - change
    work[pl.ds(first, b), :] = rows


def kernel(
    mom_hbm, grad_hbm, rf_hbm, nm, rr, scaled_ref, nf,
    mom, rf, buf, rg, sib4, lp, zr, lf, gp, gs, gr, gsum, gr2, gg, mp, ms, ra, ra1, sa, ra2, rb, sb, rb2, rb4, mg, work, sq, sqr,
    grad, send, recv, load,
):
    f, z = lax.axis_index("fsdp"), lax.axis_index("tp")
    c, x, y = lax.rem(f, 2), lax.rem(lax.div(f, 2), NX), lax.div(f, 2 * NX)

    def wrap(v, n):
        return lax.rem(v + n, n)

    def at(dx=0, dy=0, dz=0, core=None):
        chip = wrap(y + dy, NY) * NX + wrap(x + dx, NX)
        return (chip * 2 + (c if core is None else core), wrap(z + dz, NZ))

    sibling = at(core=1 - c)
    number = itertools.count()
    started = []

    def go(src, dst, to):
        i = next(number)
        copy = pltpu.make_async_remote_copy(
            src_ref=src, dst_ref=dst, send_sem=send.at[i], recv_sem=recv.at[i], device_id=to, device_id_type=MESH
        )
        copy.start()
        started.append(copy)
        return copy

    loads = [
        pltpu.make_async_copy(src, dst, load.at[i])
        for i, (src, dst) in enumerate(((rf_hbm, rf), (mom_hbm, mom), (grad_hbm, grad)))
    ]
    for copy in loads:
        copy.start()
    peers = [sibling] + [at(dx=e) for e in range(1, NX)] + [at(dy=e) for e in range(1, NY)]
    peers += [at(dz=e) for e in range(1, NZ)]
    barrier = pltpu.get_barrier_semaphore()
    for peer in peers:
        pl.semaphore_signal(barrier, inc=1, device_id=peer, device_id_type=MESH)
    loads[0].wait()
    pl.semaphore_wait(barrier, len(peers))

    class Gather:
        def __init__(self, ref):
            self.half = ref.at[c]
            self.cols_a, self.cols_b = pl.ds(0, CUT), pl.ds(CUT, REST)

        def start(self):
            half, a, b = self.half, self.cols_a, self.cols_b
            own_a, own_b = half.at[y, x, :, a], half.at[y, x, :, b]
            self.ax = [go(own_a, own_a, at(dx=e)) for e in range(1, NX)]
            self.by = {e: go(own_b, own_b, at(dy=e)) for e in OUTWARD}
            self.bx = {0: [go(own_b, own_b, at(dx=g)) for g in range(1, NX)]}

        def pass_a(self):
            for copy in self.ax:
                copy.wait_recv()
            line = self.half.at[y, :, :, self.cols_a]
            self.ay = {e: go(line, line, at(dy=e)) for e in INWARD}
            self.given = []

        def pass_b(self, e):
            self.by[e].wait_recv()
            block = self.half.at[wrap(y - e, NY), x, :, self.cols_b]
            self.bx[e] = [go(block, block, at(dx=g)) for g in range(1, NX)]

        def hand(self, e):
            for copy in self.bx[e]:
                copy.wait_recv()
            if e:
                self.ay[e].wait_recv()
            line = self.half.at[wrap(y - e, NY)]
            self.given.append(go(line, line, sibling))

        def finish(self):
            for copy in self.given:
                copy.wait_recv()

    other_cols = pl.ds(pl.multiple_of((1 - c) * HALF, 128), HALF)
    swap = go(rf.at[:, other_cols], sib4, sibling)
    swap.wait_recv()
    mine, theirs = rf[:, pl.ds(pl.multiple_of(c * HALF, 128), HALF)], sib4[...]
    rg[c, y, x, 0:4, :] = jnp.where(c == 0, mine, theirs)
    rg[c, y, x, 4:8, :] = jnp.where(c == 0, theirs, mine)
    gather = Gather(rg)
    gather.start()
    for copy in loads[1:]:
        copy.wait()
    buf[...] = mom[...] + grad[...].astype(f32)
    for e in OUTWARD[:4]:
        gather.pass_b(e)
    gather.pass_a()
    for e in OUTWARD[4:]:
        gather.pass_b(e)
    for e in (0,) + OUTWARD:
        gather.hand(e)

    def partial_left(core, total):
        def body(i, total):
            k = pl.multiple_of(i * CHUNK, 128)
            right = rg[core, :, :, :, pl.ds(k, CHUNK)].reshape(RANK, CHUNK)
            left = buf[:, pl.ds(pl.multiple_of(core * HALF + k, 128), CHUNK)]
            return total + dot(right, left, ((1,), (1,)))

        return lax.fori_loop(0, HALF // CHUNK, body, total)

    total = partial_left(c, jnp.zeros((RANK, LOCAL_ROWS), f32))
    gather.finish()
    total = partial_left(1 - c, total)

    lp[0:32] = total.reshape(32, 8, LOCAL_ROWS)
    lp[32:36] = jnp.zeros((4, 8, LOCAL_ROWS), f32)
    own_tiles = pl.ds(z * 3, 3)
    gathered = list(started)
    parts = []
    for e in AROUND:
        parts.append(go(lp.at[pl.ds(wrap(z + e, NZ) * 3, 3)], zr.at[e - 1], at(dz=e)))
    for copy in gathered:
        copy.wait_send()
    del started[: len(gathered)]
    for copy in parts:
        copy.wait_recv()
    tiles = lp[own_tiles]
    for e in range(1, NZ):
        tiles = tiles + zr[e - 1]
    lf[own_tiles] = tiles
    parts = [go(lf.at[own_tiles], lf.at[own_tiles], at(dz=e)) for e in AROUND]
    for copy in parts:
        copy.wait_recv()
    left = lf[0:32].reshape(RANK, LOCAL_ROWS)

    gram = dot(left, left, ((1,), (1,)))
    gp[0] = gram[:, :128].reshape(NY, NX, 8, 128)
    gp[1] = gram[:, 128:].reshape(NY, NX, 8, 128)
    gram_swap = go(gp.at[1 - c], gs, sibling)

    l1, l2, l3 = split3(left)
    stacked = jnp.concatenate([l1, l1, l2, l2, l1, l3], axis=1)

    def partial_rows(core, k):
        cols = pl.ds(pl.multiple_of(core * HALF + k, 128), CHUNK)
        b1, b2, b3 = split3(buf[:, cols])
        block = dot(stacked, jnp.concatenate([b1, b2, b1, b2, b3, b1], axis=0), ((1,), (0,)), None)
        mp[core, :, :, :, pl.ds(k, CHUNK)] = block.reshape(NY, NX, 8, CHUNK)

    rows_swap = []
    for k in range(0, HALF, CHUNK):
        partial_rows(1 - c, k)
        cols = pl.ds(k, CHUNK)
        rows_swap.append(go(mp.at[1 - c, :, :, :, cols], ms.at[:, :, :, cols], sibling))
    gram_swap.wait_recv()
    gs[...] = gs[...] + gp[c]
    gram_x = [go(gs.at[:, wrap(x + g, NX)], gr.at[g - 1], at(dx=g)) for g in (2, 1, 3)]
    for k in range(0, HALF, CHUNK):
        partial_rows(c, k)
    for i, k in enumerate(range(0, HALF, CHUNK)):
        rows_swap[i].wait_recv()
        cols = pl.ds(k, CHUNK)
        ms[:, :, :, cols] = ms[:, :, :, cols] + mp[c, :, :, :, cols]

    cols_a, cols_b = pl.ds(0, CUT), pl.ds(CUT, REST)
    low, high = pl.ds(CUT, PART), pl.ds(CUT + PART, REST - PART)

    def line_a(e, first=0, count=NX):
        return ms.at[wrap(y + e, NY), pl.ds(first, count), :, cols_a]

    def block_b(e, dx):
        return ms.at[wrap(y + e, NY), wrap(x + dx, NX), :, cols_b]

    order = (4, 3, 5, 2, 6, 1, 7, 0)
    first_b, direct_b, relay_b = {}, {}, {}
    for e in order:
        step = 1 if e % 2 == 0 else -1
        first_b[e] = go(block_b(e, 2), rb.at[e, 0], at(dx=step))
        direct_b[e] = go(block_b(e, -step), rb.at[e, 1], at(dx=-step))
    def relay_x(e):
        step = 1 if e % 2 == 0 else -1
        first_b[e].wait_recv()
        block = block_b(e, step)
        block[...] = block[...] + rb[e, 0]
        relay_b[e] = go(block, rb.at[e, 2], at(dx=step))

    def relay_a():
        for copy in near_a:
            copy.wait_recv()
        forward, back = wrap(y + 2, NY), wrap(y - 2, NY)
        ms[forward, :, :, cols_a] = ms[forward, :, :, cols_a] + ra1[0]
        ms[forward, 0:2, :, cols_a] = ms[forward, 0:2, :, cols_a] + ra1[2, 0:2]
        ms[back, :, :, cols_a] = ms[back, :, :, cols_a] + ra1[1]
        ms[back, 2:4, :, cols_a] = ms[back, 2:4, :, cols_a] + ra1[3, 2:4]
        far_a.update({e: go(line_a(e), ra.at[e - 1], at(dy=e)) for e in (2, 6)})

    def sum_a():
        for e in (1, 7, 2, 6):
            far_a[e].wait_recv()
        sa[...] = ms[y, :, :, cols_a] + ra[0] + ra[6] + ra[1] + ra[5]
        return [go(sa.at[wrap(x + g, NX)], ra2.at[g - 1], at(dx=g)) for g in (2, 1, 3)]

    def sum_b(e):
        direct_b[e].wait_recv()
        relay_b[e].wait_recv()
        return ms[wrap(y + e, NY), x, :, cols_b] + rb[e, 1] + rb[e, 2]

    last_b, quarter = [], []

    def send_y(e):
        sb[e] = sum_b(e)
        if e == 4:
            for part, way in ((pl.ds(0, PART), 2), (pl.ds(PART, REST - PART), -2)):
                quarter.append(go(sb.at[4, :, part], rb4.at[:, part], at(dy=way)))
        else:
            last_b.append(go(sb.at[e], rb2.at[e - 1], at(dy=e)))

    def send_two():
        for copy in quarter:
            copy.wait_recv()
        total = sum_b(2)
        sb[2, :, :PART] = total[:, :PART] + rb4[:, :PART]
        sb[2, :, PART:] = total[:, PART:]
        last_b.append(go(sb.at[2], rb2.at[1], at(dy=2)))
        total = sum_b(6)
        sb[6, :, :PART] = total[:, :PART]
        sb[6, :, PART:] = total[:, PART:] + rb4[:, PART:]
        last_b.append(go(sb.at[6], rb2.at[5], at(dy=6)))

    def gram_sum_x():
        for copy in gram_x:
            copy.wait_recv()
        part = gs[:, x]
        for g in range(1, NX):
            part = part + gr[g - 1]
        gsum[...] = part
        return [go(gsum.at[wrap(y + e, NY)], gr2.at[e - 1], at(dy=e)) for e in INWARD]

    def gram_sum_y(copies):
        for copy in copies:
            copy.wait_recv()
        part = gsum[y]
        for e in range(1, NY):
            part = part + gr2[e - 1]
        gg[c, y, x] = part
        own = gg.at[c, y, x]
        return [go(own, own, at(dy=e)) for e in INWARD]

    def gram_spread_x(copies):
        for copy in copies:
            copy.wait_recv()
        line = gg.at[c, :, x]
        return [go(line, line, at(dx=g)) for g in (2, 1, 3)]

    def gram_hand(copies):
        for copy in copies:
            copy.wait_recv()
        return go(gg.at[c], gg.at[c], sibling)

    gram_copies = gram_sum_x()
    near_a = [
        go(line_a(3), ra1.at[0], at(dy=1)),
        go(line_a(5), ra1.at[1], at(dy=-1)),
        go(line_a(4, 0, 2), ra1.at[2, pl.ds(0, 2)], at(dy=2)),
        go(line_a(4, 2, 2), ra1.at[3, pl.ds(2, 2)], at(dy=-2)),
    ]
    far_a = {e: go(line_a(e), ra.at[e - 1], at(dy=e)) for e in (1, 7)}
    for e in order[:5]:
        relay_x(e)
    gram_copies = gram_sum_y(gram_copies)
    for e in order[5:]:
        relay_x(e)
    relay_a()
    for e in (4, 3, 5, 1, 7):
        send_y(e)
    gram_copies = gram_spread_x(gram_copies)
    second_a = sum_a()
    send_two()
    part_b = sum_b(0)
    for copy in second_a:
        copy.wait_recv()
    part = sa[x]
    for g in range(1, NX):
        part = part + ra2[g - 1]
    mg[c, y, x, :, cols_a] = part
    for copy in last_b:
        copy.wait_recv()
    for e in (1, 7, 2, 6, 3, 5):
        part_b = part_b + rb2[e - 1]
    mg[c, y, x, :, cols_b] = part_b

    gather = Gather(mg)
    gather.start()
    gram_copy = gram_hand(gram_copies)
    gather.pass_b(1)
    gram_copy.wait_recv()
    work[:, :128] = gg[0].reshape(RANK, 128)
    work[:, 128:] = gg[1].reshape(RANK, 128)

    def factor(first, last):
        def body(k, carry):
            factor_step(work, k)
            return carry

        lax.fori_loop(first, last, body, 0)

    gather.pass_b(7)
    factor(0, 1)
    gather.pass_b(2)
    gather.pass_b(6)
    gather.pass_a()
    factor(1, 3)
    gather.pass_b(3)
    gather.pass_b(5)
    factor(3, 4)
    gather.pass_b(4)
    factor(4, 9)
    gather.hand(0)
    factor(9, 11)
    gather.hand(1)
    gather.hand(7)
    factor(11, 13)
    gather.hand(2)
    gather.hand(6)
    factor(13, 15)
    gather.hand(3)
    gather.hand(5)
    factor(15, 16)
    gather.hand(4)
    r = lax.broadcasted_iota(jnp.int32, (RANK, RANK), 0)
    l = lax.broadcasted_iota(jnp.int32, (RANK, RANK), 1)
    work[...] = jnp.where(l <= r, work[...], 0.0)

    def right_rows(core, squares):
        def body(i, squares):
            k = pl.multiple_of(i * CHUNK, 128)
            rows = mg[core, :, :, :, pl.ds(k, CHUNK)].reshape(RANK, CHUNK)
            top = dot(work[:128, :128], rows[:128], ((1,), (0,)))
            block = jnp.concatenate([top, dot(work[128:, :], rows, ((1,), (0,)))], axis=0)
            rr[:, pl.ds(pl.multiple_of(core * HALF + k, 128), CHUNK)] = block
            for t in range(0, CHUNK, 128):
                squares = squares + block[:, t : t + 128] * block[:, t : t + 128]
            return squares

        return lax.fori_loop(0, HALF // CHUNK, body, squares)

    squares = right_rows(c, jnp.zeros((RANK, 128), f32))
    gather.finish()
    squares = right_rows(1 - c, squares)
    sq[...] = dot(jnp.ones((8, 128), f32), squares, ((1,), (1,)))
    earlier = list(started)
    parts = [go(sq, sqr.at[e - 1], at(dz=e)) for e in AROUND]

    for copy in earlier:
        copy.wait_send()
    basis = dot(left, work[...], ((0,), (1,)))
    basis16 = basis.astype(bf16)

    def momentum_body(i, carry):
        cols = pl.ds(pl.multiple_of(i * CHUNK, 128), CHUNK)
        product = dot(basis16, rr[:, cols].astype(bf16), ((1,), (0,)), None)
        nm[:, cols] = buf[:, cols] - (1.0 - decay_rate) * product
        return carry

    lax.fori_loop(0, LOCAL // CHUNK, momentum_body, 0)
    for copy in parts:
        copy.wait_recv()
    norm = sq[...]
    for e in range(1, NZ):
        norm = norm + sqr[e - 1]
    inverse_norm = 1.0 / (jnp.sqrt(norm) + norm_eps)
    scaled = basis * (math.sqrt(ROWS * COLS / RANK) * inverse_norm[0:1, :])
    scaled_ref[...] = scaled
    chip = y * NX + x
    eight = rr[pl.ds(pl.multiple_of(chip * 8, 8), 8), :]
    r = lax.broadcasted_iota(jnp.int32, (8, RANK), 0)
    l = lax.broadcasted_iota(jnp.int32, (8, RANK), 1)
    own = jnp.sum(jnp.where(l == r + chip * 8, inverse_norm, 0.0), axis=1, keepdims=True)
    eight = eight * own
    nf[...] = jnp.where(c == 0, eight[0:4, :], eight[4:8, :])
    for copy in parts:
        copy.wait_send()


def finish(nm, rr, scaled, nf, nm_out, up_out, nf_out, up, done):
    copies = [pltpu.make_async_copy(nm, nm_out, done.at[0]), pltpu.make_async_copy(nf, nf_out, done.at[1])]
    for copy in copies:
        copy.start()
    s = scaled[...]
    s1 = s.astype(bf16)
    s2 = (s - s1.astype(f32)).astype(bf16)
    for i in range(LOCAL // WIDE):
        cols = pl.ds(i * WIDE, WIDE)
        block = rr[:, cols]
        b1 = block.astype(bf16)
        b2 = (block - b1.astype(f32)).astype(bf16)
        dims = ((1,), (0,))
        product = dot(s1, b1, dims, None) + (dot(s1, b2, dims, None) + dot(s2, b1, dims, None))
        up[:, cols] = product.astype(bf16)
        copies.append(pltpu.make_async_copy(up.at[:, cols], up_out.at[:, cols], done.at[2 + i]))
        copies[-1].start()
    for copy in copies:
        copy.wait()


def shards(momentum, gradient, right_factor):
    vmem = pl.BlockSpec(memory_space=pltpu.VMEM)
    hbm = pl.BlockSpec(memory_space=pltpu.HBM)
    scratch = [
        (LOCAL_ROWS, LOCAL),
        (4, LOCAL),
        (LOCAL_ROWS, LOCAL),
        (2, NY, NX, 8, HALF),
        (4, HALF),
        (36, 8, LOCAL_ROWS),
        (NZ - 1, 3, 8, LOCAL_ROWS),
        (36, 8, LOCAL_ROWS),
        (2, NY, NX, 8, 128),
        (NY, NX, 8, 128),
        (NX - 1, NY, 8, 128),
        (NY, 8, 128),
        (NY - 1, 8, 128),
        (2, NY, NX, 8, 128),
        (2, NY, NX, 8, HALF),
        (NY, NX, 8, HALF),
        (NY - 1, NX, 8, CUT),
        (4, NX, 8, CUT),
        (NX, 8, CUT),
        (NX - 1, 8, CUT),
        (NY, 3, 8, REST),
        (NY, 8, REST),
        (NY - 1, 8, REST),
        (8, REST),
        (2, NY, NX, 8, HALF),
        (RANK, RANK),
        (8, RANK),
        (NZ - 1, 8, RANK),
    ]
    shape = jax.ShapeDtypeStruct
    parts = pl.pallas_call(
        kernel,
        out_shape=(
            shape((LOCAL_ROWS, LOCAL), f32),
            shape((RANK, LOCAL), f32),
            shape((LOCAL_ROWS, RANK), f32),
            shape((4, LOCAL), f32),
        ),
        in_specs=[hbm] * 3,
        out_specs=(vmem,) * 4,
        scratch_shapes=[pltpu.VMEM(each, f32) for each in scratch]
        + [pltpu.VMEM((LOCAL_ROWS, LOCAL), bf16)]
        + [pltpu.SemaphoreType.DMA((COPIES,)), pltpu.SemaphoreType.DMA((COPIES,)), pltpu.SemaphoreType.DMA((3,))],
        compiler_params=pltpu.CompilerParams(collective_id=0, has_side_effects=True, vmem_limit_bytes=VMEM_LIMIT),
    )(*[pltpu.with_memory_space_constraint(a, pltpu.HBM) for a in (momentum, gradient, right_factor)])
    return pl.pallas_call(
        finish,
        out_shape=(
            shape((LOCAL_ROWS, LOCAL), f32),
            shape((LOCAL_ROWS, LOCAL), bf16),
            shape((4, LOCAL), f32),
        ),
        in_specs=[vmem] * 4,
        out_specs=(hbm,) * 3,
        scratch_shapes=[pltpu.VMEM((LOCAL_ROWS, LOCAL), bf16), pltpu.SemaphoreType.DMA((2 + LOCAL // WIDE,))],
        compiler_params=pltpu.CompilerParams(vmem_limit_bytes=16 << 20),
    )(*parts)


def solution(mesh):
    spec = P("fsdp", "tp")
    return jax.shard_map(shards, mesh=mesh, in_specs=(spec,) * 3, out_specs=(spec,) * 3, check_vma=False)
```

```python
import itertools
import math

import jax
import jax.numpy as jnp
from jax import lax
from jax.experimental import pallas as pl
from jax.experimental.pallas import tpu as pltpu
from jax.sharding import PartitionSpec as P

ROWS = 8192
COLS = 27648
RANK = 256

decay_rate = 0.9
norm_eps = 1e-08

MESH = pl.DeviceIdType.MESH
HIGHEST = lax.Precision.HIGHEST
f32 = jnp.float32
bf16 = jnp.bfloat16

NX, NY, NZ = 4, 8, 12
LOCAL_ROWS = ROWS // 64
LOCAL = COLS // NZ
HALF = LOCAL // 2
CUT = 256
REST = HALF - CUT
PART = 384
CHUNK = 384
WIDE = 768
BLOCK = 16
OUTWARD = (1, 7, 2, 6, 3, 5, 4)
INWARD = (4, 3, 5, 2, 6, 1, 7)
AROUND = (6, 5, 7, 4, 8, 3, 9, 2, 10, 1, 11)
COPIES = 384
VMEM_LIMIT = 32 << 20


def dot(a, b, dims, precision=HIGHEST):
    return lax.dot_general(a, b, (dims, ((), ())), precision=precision, preferred_element_type=f32)


def split3(a):
    first = a.astype(bf16)
    rest = a - first.astype(f32)
    second = rest.astype(bf16)
    third = (rest - second.astype(f32)).astype(bf16)
    return first, second, third


def factor_step(work, k):
    b, n = BLOCK, RANK
    first = pl.multiple_of(k * b, b)
    rows = work[pl.ds(first, b), :]
    lane = lax.broadcasted_iota(jnp.int32, (b, n), 1)
    row = lax.broadcasted_iota(jnp.int32, (b, n), 0)
    row128 = lax.broadcasted_iota(jnp.int32, (b, 128), 0)
    here = jnp.where(first >= 128, rows[:, 128:], rows[:, :128])
    here = pltpu.roll(here, lax.rem(128 - lax.rem(first, 128), 128), 1)
    column = [jnp.broadcast_to(here[:, j : j + 1], (b, 128)) for j in range(b)]
    inside = (lane >= first) & (lane < first + b)
    rows = jnp.where(inside, jnp.where(lane - first == row, 1.0, 0.0), rows)
    low, high = rows[:, :128], rows[:, 128:]
    pivots = jnp.ones((b, 128), f32)
    for j in range(b):
        pivot = column[j][j : j + 1, :]
        scaled = jnp.where(row128 > j, column[j] * (1.0 / pivot), 0.0)
        pivots = jnp.where(row128 == j, pivot, pivots)
        for i in range(j + 1, b):
            column[i] = column[i] - scaled * column[i][j : j + 1, :]
        low = low - scaled * low[j : j + 1, :]
        high = high - scaled * high[j : j + 1, :]
    scale = lax.rsqrt(pivots)
    rows = jnp.concatenate([low * scale, high * scale], axis=1)
    ahead = jnp.where(lane >= first + b, rows, 0.0)
    a1, a2, a3 = split3(ahead)
    r1, r2, r3 = split3(rows)
    change = dot(
        jnp.concatenate([a1, a1, a2, a2, a1, a3], axis=0),
        jnp.concatenate([r1, r2, r1, r2, r3, r1], axis=0),
        ((0,), (0,)),
        None,
    )
    lanes = lax.broadcasted_iota(jnp.int32, (n, n), 1)
    work[...] = jnp.where((lanes >= first) & (lanes < first + b), 0.0, work[...]) - change
    work[pl.ds(first, b), :] = rows


def kernel(
    mom_hbm, grad_hbm, rf_hbm, nm, rr, scaled_ref, nf,
    mom, rf, buf, rg, sib4, lp, zr, lf, gp, gs, gr, gsum, gr2, gg, mp, ms, ra, ra1, sa, ra2, rb, sb, rb2, rb4, mg, work, sq, sqr,
    grad, send, recv, load,
):
    f, z = lax.axis_index("fsdp"), lax.axis_index("tp")
    c, x, y = lax.rem(f, 2), lax.rem(lax.div(f, 2), NX), lax.div(f, 2 * NX)

    def wrap(v, n):
        return lax.rem(v + n, n)

    def at(dx=0, dy=0, dz=0, core=None):
        chip = wrap(y + dy, NY) * NX + wrap(x + dx, NX)
        return (chip * 2 + (c if core is None else core), wrap(z + dz, NZ))

    sibling = at(core=1 - c)
    number = itertools.count()
    started = []

    def go(src, dst, to):
        i = next(number)
        copy = pltpu.make_async_remote_copy(
            src_ref=src, dst_ref=dst, send_sem=send.at[i], recv_sem=recv.at[i], device_id=to, device_id_type=MESH
        )
        copy.start()
        started.append(copy)
        return copy

    loads = [
        pltpu.make_async_copy(src, dst, load.at[i])
        for i, (src, dst) in enumerate(((rf_hbm, rf), (mom_hbm, mom), (grad_hbm, grad)))
    ]
    for copy in loads:
        copy.start()
    peers = [sibling] + [at(dx=e) for e in range(1, NX)] + [at(dy=e) for e in range(1, NY)]
    peers += [at(dz=e) for e in range(1, NZ)]
    barrier = pltpu.get_barrier_semaphore()
    for peer in peers:
        pl.semaphore_signal(barrier, inc=1, device_id=peer, device_id_type=MESH)
    loads[0].wait()
    pl.semaphore_wait(barrier, len(peers))

    class Gather:
        def __init__(self, ref):
            self.half = ref.at[c]
            self.cols_a, self.cols_b = pl.ds(0, CUT), pl.ds(CUT, REST)

        def start(self):
            half, a, b = self.half, self.cols_a, self.cols_b
            own_a, own_b = half.at[y, x, :, a], half.at[y, x, :, b]
            self.ax = [go(own_a, own_a, at(dx=e)) for e in range(1, NX)]
            self.by = {e: go(own_b, own_b, at(dy=e)) for e in OUTWARD}
            self.bx = {0: [go(own_b, own_b, at(dx=g)) for g in range(1, NX)]}

        def pass_a(self):
            for copy in self.ax:
                copy.wait_recv()
            line = self.half.at[y, :, :, self.cols_a]
            self.ay = {e: go(line, line, at(dy=e)) for e in INWARD}
            self.given = []

        def pass_b(self, e):
            self.by[e].wait_recv()
            block = self.half.at[wrap(y - e, NY), x, :, self.cols_b]
            self.bx[e] = [go(block, block, at(dx=g)) for g in range(1, NX)]

        def hand(self, e):
            for copy in self.bx[e]:
                copy.wait_recv()
            if e:
                self.ay[e].wait_recv()
            line = self.half.at[wrap(y - e, NY)]
            self.given.append(go(line, line, sibling))

        def finish(self):
            for copy in self.given:
                copy.wait_recv()

    other_cols = pl.ds(pl.multiple_of((1 - c) * HALF, 128), HALF)
    swap = go(rf.at[:, other_cols], sib4, sibling)
    swap.wait_recv()
    mine, theirs = rf[:, pl.ds(pl.multiple_of(c * HALF, 128), HALF)], sib4[...]
    rg[c, y, x, 0:4, :] = jnp.where(c == 0, mine, theirs)
    rg[c, y, x, 4:8, :] = jnp.where(c == 0, theirs, mine)
    gather = Gather(rg)
    gather.start()
    for copy in loads[1:]:
        copy.wait()
    buf[...] = mom[...] + grad[...].astype(f32)
    for e in OUTWARD[:4]:
        gather.pass_b(e)
    gather.pass_a()
    for e in OUTWARD[4:]:
        gather.pass_b(e)
    for e in (0,) + OUTWARD:
        gather.hand(e)

    def partial_left(core, total):
        def body(i, total):
            k = pl.multiple_of(i * CHUNK, 128)
            right = rg[core, :, :, :, pl.ds(k, CHUNK)].reshape(RANK, CHUNK)
            left = buf[:, pl.ds(pl.multiple_of(core * HALF + k, 128), CHUNK)]
            return total + dot(right, left, ((1,), (1,)))

        return lax.fori_loop(0, HALF // CHUNK, body, total)

    total = partial_left(c, jnp.zeros((RANK, LOCAL_ROWS), f32))
    gather.finish()
    total = partial_left(1 - c, total)

    lp[0:32] = total.reshape(32, 8, LOCAL_ROWS)
    lp[32:36] = jnp.zeros((4, 8, LOCAL_ROWS), f32)
    own_tiles = pl.ds(z * 3, 3)
    gathered = list(started)
    parts = []
    for e in AROUND:
        parts.append(go(lp.at[pl.ds(wrap(z + e, NZ) * 3, 3)], zr.at[e - 1], at(dz=e)))
    for copy in gathered:
        copy.wait_send()
    del started[: len(gathered)]
    for copy in parts:
        copy.wait_recv()
    tiles = lp[own_tiles]
    for e in range(1, NZ):
        tiles = tiles + zr[e - 1]
    lf[own_tiles] = tiles
    parts = [go(lf.at[own_tiles], lf.at[own_tiles], at(dz=e)) for e in AROUND]
    for copy in parts:
        copy.wait_recv()
    left = lf[0:32].reshape(RANK, LOCAL_ROWS)

    gram = dot(left, left, ((1,), (1,)))
    gp[0] = gram[:, :128].reshape(NY, NX, 8, 128)
    gp[1] = gram[:, 128:].reshape(NY, NX, 8, 128)
    gram_swap = go(gp.at[1 - c], gs, sibling)

    l1, l2, l3 = split3(left)
    stacked = jnp.concatenate([l1, l1, l2, l2, l1, l3], axis=1)

    def partial_rows(core, k):
        cols = pl.ds(pl.multiple_of(core * HALF + k, 128), CHUNK)
        b1, b2, b3 = split3(buf[:, cols])
        block = dot(stacked, jnp.concatenate([b1, b2, b1, b2, b3, b1], axis=0), ((1,), (0,)), None)
        mp[core, :, :, :, pl.ds(k, CHUNK)] = block.reshape(NY, NX, 8, CHUNK)

    rows_swap = []
    for k in range(0, HALF, CHUNK):
        partial_rows(1 - c, k)
        cols = pl.ds(k, CHUNK)
        rows_swap.append(go(mp.at[1 - c, :, :, :, cols], ms.at[:, :, :, cols], sibling))
    gram_swap.wait_recv()
    gs[...] = gs[...] + gp[c]
    gram_x = [go(gs.at[:, wrap(x + g, NX)], gr.at[g - 1], at(dx=g)) for g in (2, 1, 3)]
    for k in range(0, HALF, CHUNK):
        partial_rows(c, k)
    for i, k in enumerate(range(0, HALF, CHUNK)):
        rows_swap[i].wait_recv()
        cols = pl.ds(k, CHUNK)
        ms[:, :, :, cols] = ms[:, :, :, cols] + mp[c, :, :, :, cols]

    cols_a, cols_b = pl.ds(0, CUT), pl.ds(CUT, REST)
    low, high = pl.ds(CUT, PART), pl.ds(CUT + PART, REST - PART)

    def line_a(e, first=0, count=NX):
        return ms.at[wrap(y + e, NY), pl.ds(first, count), :, cols_a]

    def block_b(e, dx):
        return ms.at[wrap(y + e, NY), wrap(x + dx, NX), :, cols_b]

    order = (4, 3, 5, 2, 6, 1, 7, 0)
    first_b, direct_b, relay_b = {}, {}, {}
    for e in order:
        step = 1 if e % 2 == 0 else -1
        first_b[e] = go(block_b(e, 2), rb.at[e, 0], at(dx=step))
        direct_b[e] = go(block_b(e, -step), rb.at[e, 1], at(dx=-step))
    def relay_x(e):
        step = 1 if e % 2 == 0 else -1
        first_b[e].wait_recv()
        block = block_b(e, step)
        block[...] = block[...] + rb[e, 0]
        relay_b[e] = go(block, rb.at[e, 2], at(dx=step))

    def relay_a():
        for copy in near_a:
            copy.wait_recv()
        forward, back = wrap(y + 2, NY), wrap(y - 2, NY)
        ms[forward, :, :, cols_a] = ms[forward, :, :, cols_a] + ra1[0]
        ms[forward, 0:2, :, cols_a] = ms[forward, 0:2, :, cols_a] + ra1[2, 0:2]
        ms[back, :, :, cols_a] = ms[back, :, :, cols_a] + ra1[1]
        ms[back, 2:4, :, cols_a] = ms[back, 2:4, :, cols_a] + ra1[3, 2:4]
        far_a.update({e: go(line_a(e), ra.at[e - 1], at(dy=e)) for e in (2, 6)})

    def sum_a():
        for e in (1, 7, 2, 6):
            far_a[e].wait_recv()
        sa[...] = ms[y, :, :, cols_a] + ra[0] + ra[6] + ra[1] + ra[5]
        return [go(sa.at[wrap(x + g, NX)], ra2.at[g - 1], at(dx=g)) for g in (2, 1, 3)]

    def sum_b(e):
        direct_b[e].wait_recv()
        relay_b[e].wait_recv()
        return ms[wrap(y + e, NY), x, :, cols_b] + rb[e, 1] + rb[e, 2]

    last_b, quarter = [], []

    def send_y(e):
        sb[e] = sum_b(e)
        if e == 4:
            for part, way in ((pl.ds(0, PART), 2), (pl.ds(PART, REST - PART), -2)):
                quarter.append(go(sb.at[4, :, part], rb4.at[:, part], at(dy=way)))
        else:
            last_b.append(go(sb.at[e], rb2.at[e - 1], at(dy=e)))

    def send_two():
        for copy in quarter:
            copy.wait_recv()
        total = sum_b(2)
        sb[2, :, :PART] = total[:, :PART] + rb4[:, :PART]
        sb[2, :, PART:] = total[:, PART:]
        last_b.append(go(sb.at[2], rb2.at[1], at(dy=2)))
        total = sum_b(6)
        sb[6, :, :PART] = total[:, :PART]
        sb[6, :, PART:] = total[:, PART:] + rb4[:, PART:]
        last_b.append(go(sb.at[6], rb2.at[5], at(dy=6)))

    def gram_sum_x():
        for copy in gram_x:
            copy.wait_recv()
        part = gs[:, x]
        for g in range(1, NX):
            part = part + gr[g - 1]
        gsum[...] = part
        return [go(gsum.at[wrap(y + e, NY)], gr2.at[e - 1], at(dy=e)) for e in INWARD]

    def gram_sum_y(copies):
        for copy in copies:
            copy.wait_recv()
        part = gsum[y]
        for e in range(1, NY):
            part = part + gr2[e - 1]
        gg[c, y, x] = part
        own = gg.at[c, y, x]
        return [go(own, own, at(dy=e)) for e in INWARD]

    def gram_spread_x(copies):
        for copy in copies:
            copy.wait_recv()
        line = gg.at[c, :, x]
        return [go(line, line, at(dx=g)) for g in (2, 1, 3)]

    def gram_hand(copies):
        for copy in copies:
            copy.wait_recv()
        return go(gg.at[c], gg.at[c], sibling)

    gram_copies = gram_sum_x()
    near_a = [
        go(line_a(3), ra1.at[0], at(dy=1)),
        go(line_a(5), ra1.at[1], at(dy=-1)),
        go(line_a(4, 0, 2), ra1.at[2, pl.ds(0, 2)], at(dy=2)),
        go(line_a(4, 2, 2), ra1.at[3, pl.ds(2, 2)], at(dy=-2)),
    ]
    far_a = {e: go(line_a(e), ra.at[e - 1], at(dy=e)) for e in (1, 7)}
    for e in order[:5]:
        relay_x(e)
    gram_copies = gram_sum_y(gram_copies)
    for e in order[5:]:
        relay_x(e)
    relay_a()
    for e in (4, 3, 5, 1, 7):
        send_y(e)
    gram_copies = gram_spread_x(gram_copies)
    second_a = sum_a()
    send_two()
    part_b = sum_b(0)
    for copy in second_a:
        copy.wait_recv()
    part = sa[x]
    for g in range(1, NX):
        part = part + ra2[g - 1]
    mg[c, y, x, :, cols_a] = part
    for copy in last_b:
        copy.wait_recv()
    for e in (1, 7, 2, 6, 3, 5):
        part_b = part_b + rb2[e - 1]
    mg[c, y, x, :, cols_b] = part_b

    gather = Gather(mg)
    gather.start()
    gram_copy = gram_hand(gram_copies)
    gather.pass_b(1)
    gram_copy.wait_recv()
    work[:, :128] = gg[0].reshape(RANK, 128)
    work[:, 128:] = gg[1].reshape(RANK, 128)

    def factor(first, last):
        def body(k, carry):
            factor_step(work, k)
            return carry

        lax.fori_loop(first, last, body, 0)

    gather.pass_b(7)
    factor(0, 1)
    gather.pass_b(2)
    gather.pass_b(6)
    gather.pass_a()
    factor(1, 3)
    gather.pass_b(3)
    gather.pass_b(5)
    factor(3, 4)
    gather.pass_b(4)
    factor(4, 9)
    gather.hand(0)
    factor(9, 11)
    gather.hand(1)
    gather.hand(7)
    factor(11, 13)
    gather.hand(2)
    gather.hand(6)
    factor(13, 15)
    gather.hand(3)
    gather.hand(5)
    factor(15, 16)
    gather.hand(4)
    r = lax.broadcasted_iota(jnp.int32, (RANK, RANK), 0)
    l = lax.broadcasted_iota(jnp.int32, (RANK, RANK), 1)
    work[...] = jnp.where(l <= r, work[...], 0.0)

    def right_rows(core, squares):
        def body(i, squares):
            k = pl.multiple_of(i * CHUNK, 128)
            rows = mg[core, :, :, :, pl.ds(k, CHUNK)].reshape(RANK, CHUNK)
            top = dot(work[:128, :128], rows[:128], ((1,), (0,)))
            block = jnp.concatenate([top, dot(work[128:, :], rows, ((1,), (0,)))], axis=0)
            rr[:, pl.ds(pl.multiple_of(core * HALF + k, 128), CHUNK)] = block
            for t in range(0, CHUNK, 128):
                squares = squares + block[:, t : t + 128] * block[:, t : t + 128]
            return squares

        return lax.fori_loop(0, HALF // CHUNK, body, squares)

    squares = right_rows(c, jnp.zeros((RANK, 128), f32))
    gather.finish()
    squares = right_rows(1 - c, squares)
    sq[...] = dot(jnp.ones((8, 128), f32), squares, ((1,), (1,)))[0:1, :]
    earlier = list(started)
    parts = [go(sq, sqr.at[e - 1], at(dz=e)) for e in AROUND]

    for copy in earlier:
        copy.wait_send()
    basis = dot(left, work[...], ((0,), (1,)))
    basis16 = basis.astype(bf16)

    def momentum_body(i, carry):
        cols = pl.ds(pl.multiple_of(i * CHUNK, 128), CHUNK)
        product = dot(basis16, rr[:, cols].astype(bf16), ((1,), (0,)), None)
        nm[:, cols] = buf[:, cols] - (1.0 - decay_rate) * product
        return carry

    lax.fori_loop(0, LOCAL // CHUNK, momentum_body, 0)
    for copy in parts:
        copy.wait_recv()
    norm = sq[...]
    for e in range(1, NZ):
        norm = norm + sqr[e - 1]
    inverse_norm = 1.0 / (jnp.sqrt(norm) + norm_eps)
    scaled = basis * (math.sqrt(ROWS * COLS / RANK) * inverse_norm)
    scaled_ref[...] = scaled
    chip = y * NX + x
    eight = rr[pl.ds(pl.multiple_of(chip * 8, 8), 8), :]
    r = lax.broadcasted_iota(jnp.int32, (8, RANK), 0)
    l = lax.broadcasted_iota(jnp.int32, (8, RANK), 1)
    own = jnp.sum(jnp.where(l == r + chip * 8, inverse_norm, 0.0), axis=1, keepdims=True)
    eight = eight * own
    nf[...] = jnp.where(c == 0, eight[0:4, :], eight[4:8, :])
    for copy in parts:
        copy.wait_send()


def finish(nm, rr, scaled, nf, nm_out, up_out, nf_out, up, done):
    copies = [pltpu.make_async_copy(nm, nm_out, done.at[0]), pltpu.make_async_copy(nf, nf_out, done.at[1])]
    for copy in copies:
        copy.start()
    s = scaled[...]
    s1 = s.astype(bf16)
    s2 = (s - s1.astype(f32)).astype(bf16)
    for i in range(LOCAL // WIDE):
        cols = pl.ds(i * WIDE, WIDE)
        block = rr[:, cols]
        b1 = block.astype(bf16)
        b2 = (block - b1.astype(f32)).astype(bf16)
        dims = ((1,), (0,))
        product = dot(s1, b1, dims, None) + (dot(s1, b2, dims, None) + dot(s2, b1, dims, None))
        up[:, cols] = product.astype(bf16)
        copies.append(pltpu.make_async_copy(up.at[:, cols], up_out.at[:, cols], done.at[2 + i]))
        copies[-1].start()
    for copy in copies:
        copy.wait()


def shards(momentum, gradient, right_factor):
    vmem = pl.BlockSpec(memory_space=pltpu.VMEM)
    hbm = pl.BlockSpec(memory_space=pltpu.HBM)
    scratch = [
        (LOCAL_ROWS, LOCAL),
        (4, LOCAL),
        (LOCAL_ROWS, LOCAL),
        (2, NY, NX, 8, HALF),
        (4, HALF),
        (36, 8, LOCAL_ROWS),
        (NZ - 1, 3, 8, LOCAL_ROWS),
        (36, 8, LOCAL_ROWS),
        (2, NY, NX, 8, 128),
        (NY, NX, 8, 128),
        (NX - 1, NY, 8, 128),
        (NY, 8, 128),
        (NY - 1, 8, 128),
        (2, NY, NX, 8, 128),
        (2, NY, NX, 8, HALF),
        (NY, NX, 8, HALF),
        (NY - 1, NX, 8, CUT),
        (4, NX, 8, CUT),
        (NX, 8, CUT),
        (NX - 1, 8, CUT),
        (NY, 3, 8, REST),
        (NY, 8, REST),
        (NY - 1, 8, REST),
        (8, REST),
        (2, NY, NX, 8, HALF),
        (RANK, RANK),
        (1, RANK),
        (NZ - 1, 1, RANK),
    ]
    shape = jax.ShapeDtypeStruct
    parts = pl.pallas_call(
        kernel,
        out_shape=(
            shape((LOCAL_ROWS, LOCAL), f32),
            shape((RANK, LOCAL), f32),
            shape((LOCAL_ROWS, RANK), f32),
            shape((4, LOCAL), f32),
        ),
        in_specs=[hbm] * 3,
        out_specs=(vmem,) * 4,
        scratch_shapes=[pltpu.VMEM(each, f32) for each in scratch]
        + [pltpu.VMEM((LOCAL_ROWS, LOCAL), bf16)]
        + [pltpu.SemaphoreType.DMA((COPIES,)), pltpu.SemaphoreType.DMA((COPIES,)), pltpu.SemaphoreType.DMA((3,))],
        compiler_params=pltpu.CompilerParams(collective_id=0, has_side_effects=True, vmem_limit_bytes=VMEM_LIMIT),
    )(*[pltpu.with_memory_space_constraint(a, pltpu.HBM) for a in (momentum, gradient, right_factor)])
    return pl.pallas_call(
        finish,
        out_shape=(
            shape((LOCAL_ROWS, LOCAL), f32),
            shape((LOCAL_ROWS, LOCAL), bf16),
            shape((4, LOCAL), f32),
        ),
        in_specs=[vmem] * 4,
        out_specs=(hbm,) * 3,
        scratch_shapes=[pltpu.VMEM((LOCAL_ROWS, LOCAL), bf16), pltpu.SemaphoreType.DMA((2 + LOCAL // WIDE,))],
        compiler_params=pltpu.CompilerParams(vmem_limit_bytes=16 << 20),
    )(*parts)


def solution(mesh):
    spec = P("fsdp", "tp")
    return jax.shard_map(shards, mesh=mesh, in_specs=(spec,) * 3, out_specs=(spec,) * 3, check_vma=False)
```
